32 devices in a mesh: gx: 4 (over z), gy: 4 (over x, core), gz: 2 (over y).
Axes of the slice: x: 2, y: 2, z: 4, core: 2. Of those that a mesh axis runs over, the one named last changes fastest.
Arguments:
- source: float32 [3, 64, 2048], P(None, 'gx', ('gy', 'gz')), may hold values from -6 to 6
- coef_x: float32 [64, 2048], P('gx', ('gy', 'gz')), may hold values from 0.2 to 5
- coef_y: float32 [64, 2048], P('gx', ('gy', 'gz')), may hold values from 0.2 to 5
- coef_z: float32 [64, 2048], P('gx', ('gy', 'gz')), may hold values from 0.2 to 5
- absorb: float32 [64, 2048], P('gx', ('gy', 'gz')), may hold values from 0.05 to 0.5
Outputs:
- correction: float32 [3, 64, 2048], P(None, 'gx', ('gy', 'gz'))
The draws below stay inside these ranges and needn't reach their ends.
All inputs are finite; a program needn't handle non-finite values.
Results may differ from the reference program's by a relative error of at most 0.0001.
Values sent between devices are 32-bit elements; how exact they have to be, the bound alone decides.
A program may use at most 64 MiB of HBM per device.

```python
import math
import jax
import jax.numpy as jnp
from jax import lax

LEVELS = 5
NU = 3
KC = 8
NRHS = 3
C = 16
NX = 64
NYZ = 2048
N_GY = 4
N_GZ = 2


def steps_of(key, dims, split, low, high):
    def one(axis_at, shards_of):
        steps = jax.random.uniform(jax.random.fold_in(jax.random.fold_in(key, 6), axis_at), (shards_of,), jnp.float32, low / len(split), high / len(split))
        return jnp.repeat(jnp.exp(steps), dims[axis_at] // shards_of).reshape((-1,) + (1,) * (len(dims) - axis_at - 1))

    gain = one(*split[0])
    for cut in split[1:]:
        gain = gain * one(*cut)
    return gain


def scatter_about(own_key, dims, spread, bound, pieces=(), held_as=jnp.bfloat16):
    drawn = jax.random.normal(own_key, dims, jnp.float32) * spread
    if len(pieces) > 0:
        drawn = steps_of(own_key, dims, pieces, -0.22, 0.18) * drawn
    return jnp.clip(drawn, min=-bound, max=bound).astype(held_as)


def setup_inputs(seed: int = 0) -> dict:
    streams_of = jax.random.split(jax.random.key(seed), 6)
    source = scatter_about(streams_of[0], (NRHS, NX, NYZ), 1.0, 6.0, ((1, 4), (2, 8)), jnp.float32)
    coef_x = jnp.clip(jnp.exp(math.log(5.0) - 3.218876 * jax.random.uniform(streams_of[1], (NX, NYZ), jnp.float32) ** steps_of(streams_of[1], (NX, NYZ), ((0, 4), (1, 8)), -0.2, 0.2)), 0.2, 5.0)
    coef_y = jnp.clip(jnp.exp(math.log(5.0) - 3.218876 * jax.random.uniform(streams_of[2], (NX, NYZ), jnp.float32) ** steps_of(streams_of[2], (NX, NYZ), ((0, 4), (1, 8)), -0.2, 0.2)), 0.2, 5.0)
    coef_z = jnp.clip(jnp.exp(math.log(5.0) - 3.218876 * jax.random.uniform(streams_of[3], (NX, NYZ), jnp.float32) ** steps_of(streams_of[3], (NX, NYZ), ((0, 4), (1, 8)), -0.2, 0.2)), 0.2, 5.0)
    absorb = jnp.clip(jnp.exp(math.log(0.5) - 2.3025851 * jax.random.uniform(streams_of[4], (NX, NYZ), jnp.float32) ** steps_of(streams_of[4], (NX, NYZ), ((0, 4), (1, 8)), -0.2, 0.2)), 0.05, 0.5)
    return {"source": source, "coef_x": coef_x, "coef_y": coef_y, "coef_z": coef_z, "absorb": absorb}


OMEGA = 0.8


def to_grid(array):
    lead = array.shape[:-2]
    n = len(lead)
    blocks = array.reshape(lead + (NX, N_GY, N_GZ, C, C))
    blocks = jnp.moveaxis(blocks, n + 3, n + 2)
    return blocks.reshape(lead + (NX, N_GY * C, N_GZ * C))


def from_grid(field):
    lead = field.shape[:-3]
    n = len(lead)
    blocks = field.reshape(lead + (NX, N_GY, C, N_GZ, C))
    blocks = jnp.moveaxis(blocks, n + 3, n + 2)
    return blocks.reshape(lead + (NX, N_GY * N_GZ * C * C))


def upper_of(coef, axis):
    rest = lax.slice_in_dim(coef, 1, coef.shape[axis], axis=axis)
    zero = jnp.zeros_like(lax.slice_in_dim(coef, 0, 1, axis=axis))
    return jnp.concatenate([rest, zero], axis=axis)


def level_terms(coef_x, coef_y, coef_z, absorb, upper_x, upper_y, upper_z):
    diag = coef_x + upper_x + coef_y + upper_y + coef_z + upper_z + absorb
    return (coef_x, upper_x, coef_y, upper_y, coef_z, upper_z, absorb, diag)


def apply_padded(padded, terms):
    coef_x, upper_x, coef_y, upper_y, coef_z, upper_z, absorb, diag = terms
    centre = padded[..., 1:-1, 1:-1, 1:-1]
    out = coef_x * (centre - padded[..., :-2, 1:-1, 1:-1])
    out = out + upper_x * (centre - padded[..., 2:, 1:-1, 1:-1])
    out = out + coef_y * (centre - padded[..., 1:-1, :-2, 1:-1])
    out = out + upper_y * (centre - padded[..., 1:-1, 2:, 1:-1])
    out = out + coef_z * (centre - padded[..., 1:-1, 1:-1, :-2])
    out = out + upper_z * (centre - padded[..., 1:-1, 1:-1, 2:])
    return out + absorb * centre


def coarsen_coef(coef, keep):
    sizes = coef.shape
    blocks = coef.reshape(sizes[0] // 2, 2, sizes[1] // 2, 2, sizes[2] // 2, 2)
    if keep == 0:
        return blocks[:, 0].sum(axis=(2, 4))
    if keep == 1:
        return blocks[:, :, :, 0].sum(axis=(1, 4))
    return blocks[:, :, :, :, :, 0].sum(axis=(1, 3))


def coarsen_cells(field):
    sizes = field.shape
    lead = sizes[:-3]
    blocks = field.reshape(lead + (sizes[-3] // 2, 2, sizes[-2] // 2, 2, sizes[-1] // 2, 2))
    n = len(lead)
    return blocks.sum(axis=(n + 1, n + 3, n + 5))


def refine_cells(field):
    n = field.ndim
    out = jnp.repeat(field, 2, axis=n - 3)
    out = jnp.repeat(out, 2, axis=n - 2)
    return jnp.repeat(out, 2, axis=n - 1)


def pad_field(field):
    return jnp.pad(field, [(0, 0)] * (field.ndim - 3) + [(1, 1), (1, 1), (1, 1)])


def sweep(field, rhs, terms):
    return field + OMEGA * (rhs - apply_padded(pad_field(field), terms)) / terms[7]


def reference(source, coef_x, coef_y, coef_z, absorb):
    source = to_grid(source)
    coef_x, coef_y, coef_z, absorb = to_grid(coef_x), to_grid(coef_y), to_grid(coef_z), to_grid(absorb)
    levels = []
    kx, ky, kz, sa = coef_x, coef_y, coef_z, absorb
    for level in range(LEVELS):
        levels.append(level_terms(kx, ky, kz, sa, upper_of(kx, 0), upper_of(ky, 1), upper_of(kz, 2)))
        if level + 1 < LEVELS:
            kx, ky, kz, sa = coarsen_coef(kx, 0), coarsen_coef(ky, 1), coarsen_coef(kz, 2), coarsen_cells(sa)

    def cycle(rhs_top):
        rhs = rhs_top
        kept = []
        for level in range(LEVELS - 1):
            terms = levels[level]
            field = jnp.zeros_like(rhs)
            for step in range(NU):
                field = sweep(field, rhs, terms)
            kept.append((field, rhs))
            rhs = coarsen_cells(rhs - apply_padded(pad_field(field), terms))
        field = jnp.zeros_like(rhs)
        for step in range(KC):
            field = sweep(field, rhs, levels[LEVELS - 1])
        for level in range(LEVELS - 2, -1, -1):
            own, rhs = kept[level]
            field = own + refine_cells(field)
            for step in range(NU):
                field = sweep(field, rhs, levels[level])
        return field

    return from_grid(lax.map(cycle, source))
```

```python
import functools

import jax
import jax.numpy as jnp
from jax import lax
from jax.experimental import pallas as pl
from jax.experimental.pallas import tpu as pltpu
from jax.sharding import PartitionSpec as P

LEVELS = 5
NU = 3
KC = 8


OMEGA = 0.8


def passed_along(array, axis, by):
    peers = lax.axis_size(axis)
    pairs = [(i, i + by) for i in range(peers) if 0 <= i + by < peers]
    return lax.ppermute(array, axis, pairs)


def extended(array, sides, width):
    for axis, dim in sides:
        peers, length = (lax.axis_size(axis), array.shape[dim])
        up = [(i, (i + 1) % peers) for i in range(peers - 1)]
        down = [(j, i) for i, j in up]
        last = lax.slice_in_dim(array, length - width, length, axis=dim)
        first = lax.slice_in_dim(array, 0, width, axis=dim)
        before = lax.ppermute(last, axis, up)
        after = lax.ppermute(first, axis, down)
        array = jnp.concatenate([before, array, after], axis=dim)
    return array


def level_terms(coef_x, coef_y, coef_z, absorb, upper_x, upper_y, upper_z):
    diag = coef_x + upper_x + coef_y + upper_y + coef_z + upper_z + absorb
    return (coef_x, upper_x, coef_y, upper_y, coef_z, upper_z, absorb, diag)


def apply_padded(padded, terms):
    coef_x, upper_x, coef_y, upper_y, coef_z, upper_z, absorb, diag = terms
    centre = padded[..., 1:-1, 1:-1, 1:-1]
    out = coef_x * (centre - padded[..., :-2, 1:-1, 1:-1])
    out = out + upper_x * (centre - padded[..., 2:, 1:-1, 1:-1])
    out = out + coef_y * (centre - padded[..., 1:-1, :-2, 1:-1])
    out = out + upper_y * (centre - padded[..., 1:-1, 2:, 1:-1])
    out = out + coef_z * (centre - padded[..., 1:-1, 1:-1, :-2])
    out = out + upper_z * (centre - padded[..., 1:-1, 1:-1, 2:])
    return out + absorb * centre


def coarsen_coef(coef, keep):
    sizes = coef.shape
    blocks = coef.reshape(sizes[0] // 2, 2, sizes[1] // 2, 2, sizes[2] // 2, 2)
    if keep == 0:
        return blocks[:, 0].sum(axis=(2, 4))
    if keep == 1:
        return blocks[:, :, :, 0].sum(axis=(1, 4))
    return blocks[:, :, :, :, :, 0].sum(axis=(1, 3))


def coarsen_cells(field):
    sizes = field.shape
    lead = sizes[:-3]
    blocks = field.reshape(lead + (sizes[-3] // 2, 2, sizes[-2] // 2, 2, sizes[-1] // 2, 2))
    n = len(lead)
    return blocks.sum(axis=(n + 1, n + 3, n + 5))


def refine_cells(field):
    n = field.ndim
    out = jnp.repeat(field, 2, axis=n - 3)
    out = jnp.repeat(out, 2, axis=n - 2)
    return jnp.repeat(out, 2, axis=n - 1)


def shard_terms(kx, ky, kz, absorb):
    plane_x = passed_along(kx[:1], "gx", -1)
    plane_y = passed_along(ky[:, :1], "gy", -1)
    plane_z = passed_along(kz[:, :, :1], "gz", -1)
    upper_x = jnp.concatenate([kx[1:], plane_x], axis=0)
    upper_y = jnp.concatenate([ky[:, 1:], plane_y], axis=1)
    upper_z = jnp.concatenate([kz[:, :, 1:], plane_z], axis=2)
    return level_terms(kx, ky, kz, absorb, upper_x, upper_y, upper_z)


def padded_shard(field):
    return extended(field, (("gx", 1), ("gy", 2), ("gz", 3)), 1)


def smooth(field, rhs, terms, count, fresh):
    for step in range(count):
        if fresh and step == 0:
            field = OMEGA * rhs / terms[7]
        else:
            field = field + OMEGA * (rhs - apply_padded(padded_shard(field), terms)) / terms[7]
    return field


def body(source, coef_x, coef_y, coef_z, absorb):
    side = coef_x.shape[0]
    batch = source.shape[0]
    source = source.reshape(batch, side, side, side)
    coef_x = coef_x.reshape(side, side, side)
    coef_y = coef_y.reshape(side, side, side)
    coef_z = coef_z.reshape(side, side, side)
    absorb = absorb.reshape(side, side, side)
    shapes = []
    kx, ky, kz, sa = (coef_x, coef_y, coef_z, absorb)
    for level in range(LEVELS):
        shapes.append((kx, ky, kz, sa))
        if level + 1 < LEVELS:
            kx, ky, kz, sa = (
                coarsen_coef(kx, 0),
                coarsen_coef(ky, 1),
                coarsen_coef(kz, 2),
                coarsen_cells(sa),
            )
    start = LEVELS - 1
    levels = [shard_terms(*shapes[level]) for level in range(start)]
    rhs = source
    kept = []
    for level in range(start):
        terms = levels[level]
        field = smooth(rhs, rhs, terms, NU, True)
        kept.append((field, rhs))
        rhs = coarsen_cells(rhs - apply_padded(padded_shard(field), terms))
    coarse_terms = shard_terms(*shapes[LEVELS - 1])
    field = smooth(rhs, rhs, coarse_terms, KC, True)
    for level in range(start - 1, -1, -1):
        own, rhs = kept[level]
        field = own + refine_cells(field)
        field = smooth(field, rhs, levels[level], NU, False)
    return field.reshape(batch, side, side * side)


MESH_AXES = ("gx", "gy", "gz")
GATHER_CELLS = 32768
F32 = jnp.float32
BF16 = jnp.bfloat16


def iota2(shape, dim):
    return lax.broadcasted_iota(jnp.int32, shape, dim)


def split_dot(values, selector, transposed=False):
    dims = (((1,), (1,)), ((), ())) if transposed else (((1,), (0,)), ((), ()))
    high = values.astype(BF16)
    rest = values - high.astype(F32)
    mid = rest.astype(BF16)
    low = (rest - mid.astype(F32)).astype(BF16)

    def one(part):
        return lax.dot_general(part, selector, dims, preferred_element_type=F32)

    return one(high) + (one(mid) + one(low))


def selector(lanes, nz, cells, coarse_nz, offset):
    fine = iota2((lanes, 128), 0)
    coarse = iota2((lanes, 128), 1)
    target = (fine // nz // 2) * coarse_nz + (fine % nz) // 2 + offset
    hit = jnp.where((target == coarse) & (fine < cells), 1.0, 0.0)
    return hit.astype(BF16)


def paired_rows(tmp, rows):
    return tmp[pl.ds(0, rows, stride=2), :], tmp[pl.ds(1, rows, stride=2), :]


def doubled_rows(tmp, values):
    rows = values.shape[0]
    tmp[pl.ds(0, rows, stride=2), :] = values
    tmp[pl.ds(1, rows, stride=2), :] = values
    return tmp[0 : 2 * rows, :]


def roll(values, by, axis):
    return pltpu.roll(values, by % values.shape[axis], axis)


def stencil(field, terms, nz):
    lanes = field.shape[1]
    rows = field.shape[0]
    out = terms[0] * pltpu.roll(field, 1, 0) + terms[1] * pltpu.roll(field, rows - 1, 0)
    out = out + (terms[2] * pltpu.roll(field, nz, 1) + terms[3] * pltpu.roll(field, lanes - nz, 1))
    return out + (terms[4] * pltpu.roll(field, 1, 1) + terms[5] * pltpu.roll(field, lanes - 1, 1))


def coarse_coefs(stack, sel, tmp, ny_even, nz_even):
    kx, ky, kz, sa = stack
    rows = kx.shape[0]
    joined = jnp.concatenate([kx, jnp.where(ny_even, ky, 0.0), jnp.where(nz_even, kz, 0.0), sa], axis=0)
    tmp[0 : 4 * rows, :] = split_dot(joined, sel)
    even, odd = paired_rows(tmp, 2 * rows)
    half = rows // 2
    first = even[:half]
    rest = even[half:] + odd[half:]
    return first, rest[:half], rest[half : 2 * half], rest[2 * half :]


def whole_terms(stack, nx, ny, nz):
    kx, ky, kz, sa = stack
    rows, lanes = kx.shape
    x = iota2((rows, lanes), 0)
    lane = iota2((rows, lanes), 1)
    y, z = lane // nz, lane % nz
    real = (x < nx) & (y < ny)
    up_x = jnp.where(x < nx - 1, pltpu.roll(kx, rows - 1, 0), 0.0)
    up_y = jnp.where(y < ny - 1, roll(ky, -nz, 1), 0.0)
    up_z = jnp.where(z < nz - 1, roll(kz, -1, 1), 0.0)
    diag = kx + up_x + ky + up_y + kz + up_z + sa
    weight = jnp.where(real, OMEGA / jnp.where(real, diag, 1.0), 0.0)
    zero = jnp.zeros_like(kx)
    return (
        jnp.where(x > 0, kx * weight, 0.0),
        jnp.where(real, up_x * weight, 0.0),
        jnp.where(y > 0, ky * weight, 0.0),
        jnp.where(real, up_y * weight, 0.0),
        jnp.where(z > 0, kz * weight, 0.0),
        jnp.where(real, up_z * weight, 0.0),
        weight,
        jnp.where(real, diag * (1.0 / OMEGA), zero),
    )


def cycle_kernel(peers, side, batch, src, kx_ref, ky_ref, kz_ref, sa_ref, out, u_s, xs, xr, yr, zs, zr,
                 cxr, cyr, czr, tmp, tile, zpart, full, kterms, t1, t2, t3, t4, ctile, czpart, cfull, back,
                 hsend, hrecv, gsend, grecv):
    gxn, gyn, gzn = peers
    gx, gy, gz = lax.axis_index("gx"), lax.axis_index("gy"), lax.axis_index("gz")
    lanes = side * side
    last = lanes - 128
    MESH = pl.DeviceIdType.MESH

    def at_x(i):
        return (i, gy, gz)

    def at_y(i):
        return (gx, i, gz)

    partner = (gx, gy, 1 - gz)
    others = [at_x(lax.rem(gx + d, gxn)) for d in range(1, gxn)]
    others += [at_y(lax.rem(gy + d, gyn)) for d in range(1, gyn)]
    others += [partner]

    xs[...] = jnp.zeros_like(xs)
    xr[...] = jnp.zeros_like(xr)
    yr[...] = jnp.zeros_like(yr)
    cxr[...] = jnp.zeros_like(cxr)
    cyr[...] = jnp.zeros_like(cyr)

    barrier = pltpu.get_barrier_semaphore()
    for peer in others:
        pl.semaphore_signal(barrier, inc=1, device_id=peer, device_id_type=MESH)
    pl.semaphore_wait(barrier, len(others))

    pending = []

    def copy(a, b, s, r, peer):
        return pltpu.make_async_remote_copy(
            src_ref=a, dst_ref=b, send_sem=s, recv_sem=r, device_id=peer, device_id_type=MESH
        )

    def start(c, when=None):
        if when is None:
            c.start()
        else:
            pl.when(when)(c.start)

    def wait(c, kind, when=None):
        run = c.wait_recv if kind == "recv" else c.wait_send
        if when is None:
            run()
        else:
            pl.when(when)(run)

    has_lo_x, has_hi_x = gx > 0, gx < gxn - 1
    has_lo_y, has_hi_y = gy > 0, gy < gyn - 1

    nk = NU * 2
    c_x = copy(kx_ref.at[0:8], cxr, hsend.at[nk, 0], hrecv.at[nk, 0], at_x(gx - 1))
    c_y = copy(ky_ref.at[:, 0:128], cyr, hsend.at[nk, 1], hrecv.at[nk, 1], at_y(gy - 1))
    c_z = copy(kz_ref, czr, hsend.at[nk, 2], hrecv.at[nk, 2], partner)
    start(c_x, has_lo_x)
    start(c_y, has_lo_y)
    start(c_z)
    pending += [(c_x, has_lo_x), (c_y, has_lo_y), (c_z, None)]

    kx, ky, kz, sa = kx_ref[...], ky_ref[...], kz_ref[...], sa_ref[...]
    x = iota2((side, lanes), 0)
    lane = iota2((side, lanes), 1)
    y, z = lane // side, lane % side
    half = side // 2
    nz1 = half * gzn
    sel0 = selector(lanes, side, lanes, nz1, gz * half)
    even_y, even_z = (y % 2) == 0, (z % 2) == 0
    coarse = coarse_coefs((kx, ky, kz, sa), sel0, tmp, even_y, even_z)
    for i in range(4):
        ctile[i] = coarse[i]

    mine_x, mine_y = pl.ds(pl.multiple_of(gx * half, half), half), pl.ds(pl.multiple_of(gy * 128, 128), 128)

    def gather_z(a, b, base):
        c = copy(a, b, gsend.at[base], grecv.at[base], partner)
        start(c)
        pending.append((c, None))
        return [c]

    def gather_x(whole, base):
        cs = []
        for d in range(1, gxn):
            ref = whole.at[:, mine_x, mine_y]
            cs.append(copy(ref, ref, gsend.at[base + d], grecv.at[base + d], at_x(lax.rem(gx + d, gxn))))
        for c in cs:
            start(c)
            pending.append((c, None))
        return cs

    def gather_y(whole, base):
        cs = []
        for d in range(1, gyn):
            ref = whole.at[:, :, mine_y]
            cs.append(
                copy(ref, ref, gsend.at[base + gxn + d], grecv.at[base + gxn + d], at_y(lax.rem(gy + d, gyn)))
            )
        for c in cs:
            start(c)
            pending.append((c, None))
        return cs

    def landed(cs):
        for c in cs:
            wait(c, "recv")

    cbase = gxn + gyn
    g = gather_z(ctile, czpart, cbase)

    wait(c_x, "recv", has_hi_x)
    wait(c_y, "recv", has_hi_y)
    wait(c_z, "recv")

    ylo_mask = (iota2((side, 128), 1) < side)
    yhi_mask = (iota2((side, 128), 1) >= 128 - side)
    first_z, last_z = z == 0, z == side - 1
    up_x = jnp.where(x == side - 1, jnp.broadcast_to(cxr[0:1, :], (side, lanes)), roll(kx, -1, 0))
    from_y = jnp.where(yhi_mask, roll(cyr[...], -side, 1), 0.0)
    up_y = roll(ky, -side, 1)
    up_y = jnp.where(y == side - 1, 0.0, up_y)
    tail = up_y[:, last:] + from_y
    up_y = tail if last == 0 else jnp.concatenate([up_y[:, :last], tail], axis=1)
    low_z = gz == 0
    from_z = jnp.where(low_z, roll(czr[...], side - 1, 1), 0.0)
    up_z = jnp.where(last_z, from_z, roll(kz, -1, 1))
    diag = kx + up_x + ky + up_y + kz + up_z + sa
    weight = OMEGA / diag
    wx, wux, wy, wuy, wz, wuz = [k * weight for k in (kx, up_x, ky, up_y, kz, up_z)]
    inner = (
        jnp.where(x > 0, wx, 0.0),
        jnp.where(x < side - 1, wux, 0.0),
        jnp.where(y > 0, wy, 0.0),
        jnp.where(y < side - 1, wuy, 0.0),
        jnp.where(first_z, 0.0, wz),
        jnp.where(last_z, 0.0, wuz),
    )
    for i in range(6):
        kterms[i] = inner[i]
    kterms[6] = weight
    kterms[7] = diag * (1.0 / OMEGA)
    kterms[8] = jnp.where((x == 0) & has_lo_x, wx, 0.0)
    kterms[9] = jnp.where(x == side - 1, wux, 0.0)
    edge_y = jnp.concatenate(
        [jnp.where(ylo_mask & has_lo_y, wy[:, :128], 0.0), jnp.where(yhi_mask, wuy[:, last:], 0.0)], axis=1
    )
    kterms[10] = edge_y
    kterms[11] = jnp.where(low_z, jnp.where(last_z, wuz, 0.0), jnp.where(first_z, wz, 0.0))

    rhs = [weight * src[r] for r in range(batch)]

    def exchange(k, fields):
        for r in range(batch):
            u_s[k, r] = fields[r]
            xs[k, 0, r : r + 1, :] = fields[r][0:1]
            xs[k, 1, r : r + 1, :] = fields[r][side - 1 : side]
        packed = None
        for r in range(batch):
            moved = pltpu.roll(fields[r], jnp.where(low_z, lanes - (side - 1 - r), side - 1 - r), 1)
            at = jnp.where(low_z, r, side - 1 - r)
            packed = moved if packed is None else jnp.where(z == at, moved, packed)
        zs[k] = packed
        x_lo = copy(xs.at[k, 0], xr.at[k, 1], hsend.at[k, 0], hrecv.at[k, 0], at_x(gx - 1))
        x_hi = copy(xs.at[k, 1], xr.at[k, 0], hsend.at[k, 1], hrecv.at[k, 1], at_x(gx + 1))
        y_lo = copy(u_s.at[k, :, :, 0:128], yr.at[k, 1], hsend.at[k, 2], hrecv.at[k, 2], at_y(gy - 1))
        y_hi = copy(u_s.at[k, :, :, last:lanes], yr.at[k, 0], hsend.at[k, 3], hrecv.at[k, 3], at_y(gy + 1))
        z_to = copy(zs.at[k], zr.at[k], hsend.at[k, 4], hrecv.at[k, 4], partner)
        sent = [(x_lo, has_lo_x), (x_hi, has_hi_x), (y_lo, has_lo_y), (y_hi, has_hi_y), (z_to, None)]
        for c, when in sent:
            start(c, when)
        pending.extend(sent)
        return [(x_lo, has_hi_x), (x_hi, has_lo_x), (y_lo, has_hi_y), (y_hi, has_lo_y), (z_to, None)]

    def moved_by(k, fields, between=None):
        incoming = exchange(k, fields)
        terms = [kterms[i] for i in range(6)]
        acc = [rhs[r] + stencil(fields[r], terms, side) for r in range(batch)]
        if between is not None:
            between()
        for c, when in incoming:
            wait(c, "recv", when)
        for r in range(batch):
            a = kterms[8] * jnp.broadcast_to(xr[k, 0, r : r + 1, :], (side, lanes))
            a = a + kterms[9] * jnp.broadcast_to(xr[k, 1, r : r + 1, :], (side, lanes))
            ys = jnp.concatenate([roll(yr[k, 0, r], side, 1), roll(yr[k, 1, r], -side, 1)], axis=1)
            a = a + kterms[10] * ys
            zv = pltpu.roll(zr[k], jnp.where(low_z, r, (lanes - r) % lanes), 1) if r else zr[k]
            a = a + kterms[11] * zv
            acc[r] = acc[r] + a
        return acc

    def sweep0(k, fields, between=None):
        acc = moved_by(k, fields, between)
        return [(1.0 - OMEGA) * fields[r] + acc[r] for r in range(batch)]

    state = {}

    def coefs_x():
        landed(g)
        for i in range(4):
            cfull[i, mine_x, mine_y] = ctile[i] + czpart[i]
        state["c"] = gather_x(cfull, cbase)

    def coefs_y():
        landed(state["c"])
        state["c"] = gather_y(cfull, cbase)

    nx1, ny1 = gxn * half, gyn * half
    dims = [(nx1 >> i, ny1 >> i, nz1 >> i) for i in range(LEVELS - 1)]
    stores = [t1, t2, t3, t4]
    sels = []

    def coefs_done():
        landed(state["c"])
        stack = tuple(cfull[i] for i in range(4))
        for i, (nx, ny, nz) in enumerate(dims):
            terms = whole_terms(stack, nx, ny, nz)
            for j in range(8):
                stores[i][j] = terms[j]
            if i + 1 < len(dims):
                rows, wide = stack[0].shape
                sel = selector(wide, nz, ny * nz, nz // 2, 0)
                sels.append(sel)
                ln = iota2((rows, wide), 1)
                nxt = coarse_coefs(stack, sel, tmp, (ln // nz) % 2 == 0, (ln % nz) % 2 == 0)
                if nxt[0].shape[0] < 8:
                    pad = jnp.zeros((8 - nxt[0].shape[0], 128), F32)
                    nxt = tuple(jnp.concatenate([a, pad], axis=0) for a in nxt)
                stack = nxt

    u = list(rhs)
    u = sweep0(0, u, coefs_x)
    u = sweep0(1, u, coefs_y)
    acc = moved_by(2, u, coefs_done)
    own0 = u
    res = jnp.concatenate([kterms[7] * (acc[r] - OMEGA * u[r]) for r in range(batch)], axis=0)
    tmp[0 : batch * side, :] = split_dot(res, sel0)
    a, b = paired_rows(tmp, batch * half)
    f1 = a + b
    for r in range(batch):
        tile[r] = f1[r * half : (r + 1) * half]
    landed(gather_z(tile, zpart, 0))
    for r in range(batch):
        full[r, mine_x, mine_y] = tile[r] + zpart[r]
    landed(gather_x(full, 0))
    landed(gather_y(full, 0))

    def sweeps(fields, wf, i, count):
        nz = dims[i][2]
        for _ in range(count):
            terms = [stores[i][j] for j in range(6)]
            fields = [
                (1.0 - OMEGA) * fields[r] + (wf[r] + stencil(fields[r], terms, nz)) for r in range(batch)
            ]
        return fields

    f = [full[r] for r in range(batch)]
    kept = []
    for i in range(LEVELS - 2):
        nz = dims[i][2]
        wf = [stores[i][6] * f[r] for r in range(batch)]
        v = sweeps(wf, wf, i, NU - 1)
        kept.append((v, wf))
        terms = [stores[i][j] for j in range(6)]
        res = [
            stores[i][7] * (wf[r] + stencil(v[r], terms, nz) - OMEGA * v[r]) for r in range(batch)
        ]
        rows = res[0].shape[0]
        tmp[0 : batch * rows, :] = split_dot(jnp.concatenate(res, axis=0), sels[i])
        a, b = paired_rows(tmp, batch * rows // 2)
        f1 = a + b
        hr = rows // 2
        f = [f1[r * hr : (r + 1) * hr] for r in range(batch)]
        if hr < 8:
            pad = jnp.zeros((8 - hr, 128), F32)
            f = [jnp.concatenate([p, pad], axis=0) for p in f]
    i = LEVELS - 2
    wf = [stores[i][6] * f[r] for r in range(batch)]
    v = sweeps(wf, wf, i, KC - 1)
    for i in range(LEVELS - 3, -1, -1):
        own, wf = kept[i]
        rows = own[0].shape[0]
        wide = doubled_rows(tmp, jnp.concatenate([v[r][: rows // 2] for r in range(batch)], axis=0))
        up = split_dot(wide, sels[i], transposed=True)
        v = [own[r] + up[r * rows : (r + 1) * rows] for r in range(batch)]
        v = sweeps(v, wf, i, NU)
    for r in range(batch):
        back[r] = v[r]
    part = jnp.concatenate([back[r, mine_x, mine_y] for r in range(batch)], axis=0)
    up = split_dot(doubled_rows(tmp, part), sel0, transposed=True)
    u = [own0[r] + up[r * side : (r + 1) * side] for r in range(batch)]
    for s in range(NU):
        u = sweep0(NU + s, u)
    for r in range(batch):
        out[r] = u[r]
    for c, when in pending:
        wait(c, "send", when)


def kernel_body(peers, source, coef_x, coef_y, coef_z, absorb):
    gxn, gyn, gzn = peers
    batch, side, lanes = source.shape
    half = side // 2
    nx1 = gxn * half
    wide = gyn * half * gzn * half
    ex = 2 * NU
    row_counts = [max(8, nx1 >> i) for i in range(LEVELS - 1)]
    scratch = [
        pltpu.VMEM((ex, batch, side, lanes), F32),
        pltpu.VMEM((ex, 2, 8, lanes), F32),
        pltpu.VMEM((ex, 2, 8, lanes), F32),
        pltpu.VMEM((ex, 2, batch, side, 128), F32),
        pltpu.VMEM((ex, side, lanes), F32),
        pltpu.VMEM((ex, side, lanes), F32),
        pltpu.VMEM((8, lanes), F32),
        pltpu.VMEM((side, 128), F32),
        pltpu.VMEM((side, lanes), F32),
        pltpu.VMEM((4 * nx1 + 64, 128), F32),
        pltpu.VMEM((batch, half, 128), F32),
        pltpu.VMEM((batch, half, 128), F32),
        pltpu.VMEM((batch, nx1, wide), F32),
        pltpu.VMEM((12, side, lanes), F32),
        pltpu.VMEM((8, row_counts[0], wide), F32),
        pltpu.VMEM((8, row_counts[1], 128), F32),
        pltpu.VMEM((8, row_counts[2], 128), F32),
        pltpu.VMEM((8, row_counts[3], 128), F32),
        pltpu.VMEM((4, half, 128), F32),
        pltpu.VMEM((4, half, 128), F32),
        pltpu.VMEM((4, nx1, wide), F32),
        pltpu.VMEM((batch, nx1, wide), F32),
        pltpu.SemaphoreType.DMA((ex + 1, 5)),
        pltpu.SemaphoreType.DMA((ex + 1, 5)),
        pltpu.SemaphoreType.DMA((2 * (gxn + gyn),)),
        pltpu.SemaphoreType.DMA((2 * (gxn + gyn),)),
    ]
    return pl.pallas_call(
        functools.partial(cycle_kernel, peers, side, batch),
        out_shape=jax.ShapeDtypeStruct(source.shape, F32),
        in_specs=[pl.BlockSpec(memory_space=pltpu.VMEM)] * 5,
        out_specs=pl.BlockSpec(memory_space=pltpu.VMEM),
        scratch_shapes=scratch,
        compiler_params=pltpu.CompilerParams(
            collective_id=0, has_side_effects=True, vmem_limit_bytes=48 * 1024 * 1024
        ),
    )(source, coef_x, coef_y, coef_z, absorb)


def solution(mesh):
    placed = (
        P(None, "gx", ("gy", "gz")),
        P("gx", ("gy", "gz")),
        P("gx", ("gy", "gz")),
        P("gx", ("gy", "gz")),
        P("gx", ("gy", "gz")),
    )
    peers = tuple(mesh.shape[a] for a in MESH_AXES)

    def local(source, coef_x, coef_y, coef_z, absorb):
        side = source.shape[1]
        half = side // 2
        fits = peers[0] * peers[1] * peers[2] * half**3 <= GATHER_CELLS
        fits = fits and peers[2] == 2 and half * half * peers[2] == 128
        if fits:
            return kernel_body(peers, source, coef_x, coef_y, coef_z, absorb)
        return body(source, coef_x, coef_y, coef_z, absorb)

    return jax.shard_map(
        local, mesh=mesh, in_specs=placed, out_specs=P(None, "gx", ("gy", "gz")), check_vma=False
    )
```

```python
import functools

import jax
import jax.numpy as jnp
from jax import lax
from jax.experimental import pallas as pl
from jax.experimental.pallas import tpu as pltpu
from jax.sharding import PartitionSpec as P

LEVELS = 5
NU = 3
KC = 8


OMEGA = 0.8


def passed_along(array, axis, by):
    peers = lax.axis_size(axis)
    pairs = [(i, i + by) for i in range(peers) if 0 <= i + by < peers]
    return lax.ppermute(array, axis, pairs)


def extended(array, sides, width):
    for axis, dim in sides:
        peers, length = (lax.axis_size(axis), array.shape[dim])
        up = [(i, (i + 1) % peers) for i in range(peers - 1)]
        down = [(j, i) for i, j in up]
        last = lax.slice_in_dim(array, length - width, length, axis=dim)
        first = lax.slice_in_dim(array, 0, width, axis=dim)
        before = lax.ppermute(last, axis, up)
        after = lax.ppermute(first, axis, down)
        array = jnp.concatenate([before, array, after], axis=dim)
    return array


def level_terms(coef_x, coef_y, coef_z, absorb, upper_x, upper_y, upper_z):
    diag = coef_x + upper_x + coef_y + upper_y + coef_z + upper_z + absorb
    return (coef_x, upper_x, coef_y, upper_y, coef_z, upper_z, absorb, diag)


def apply_padded(padded, terms):
    coef_x, upper_x, coef_y, upper_y, coef_z, upper_z, absorb, diag = terms
    centre = padded[..., 1:-1, 1:-1, 1:-1]
    out = coef_x * (centre - padded[..., :-2, 1:-1, 1:-1])
    out = out + upper_x * (centre - padded[..., 2:, 1:-1, 1:-1])
    out = out + coef_y * (centre - padded[..., 1:-1, :-2, 1:-1])
    out = out + upper_y * (centre - padded[..., 1:-1, 2:, 1:-1])
    out = out + coef_z * (centre - padded[..., 1:-1, 1:-1, :-2])
    out = out + upper_z * (centre - padded[..., 1:-1, 1:-1, 2:])
    return out + absorb * centre


def coarsen_coef(coef, keep):
    sizes = coef.shape
    blocks = coef.reshape(sizes[0] // 2, 2, sizes[1] // 2, 2, sizes[2] // 2, 2)
    if keep == 0:
        return blocks[:, 0].sum(axis=(2, 4))
    if keep == 1:
        return blocks[:, :, :, 0].sum(axis=(1, 4))
    return blocks[:, :, :, :, :, 0].sum(axis=(1, 3))


def coarsen_cells(field):
    sizes = field.shape
    lead = sizes[:-3]
    blocks = field.reshape(lead + (sizes[-3] // 2, 2, sizes[-2] // 2, 2, sizes[-1] // 2, 2))
    n = len(lead)
    return blocks.sum(axis=(n + 1, n + 3, n + 5))


def refine_cells(field):
    n = field.ndim
    out = jnp.repeat(field, 2, axis=n - 3)
    out = jnp.repeat(out, 2, axis=n - 2)
    return jnp.repeat(out, 2, axis=n - 1)


def shard_terms(kx, ky, kz, absorb):
    plane_x = passed_along(kx[:1], "gx", -1)
    plane_y = passed_along(ky[:, :1], "gy", -1)
    plane_z = passed_along(kz[:, :, :1], "gz", -1)
    upper_x = jnp.concatenate([kx[1:], plane_x], axis=0)
    upper_y = jnp.concatenate([ky[:, 1:], plane_y], axis=1)
    upper_z = jnp.concatenate([kz[:, :, 1:], plane_z], axis=2)
    return level_terms(kx, ky, kz, absorb, upper_x, upper_y, upper_z)


def padded_shard(field):
    return extended(field, (("gx", 1), ("gy", 2), ("gz", 3)), 1)


def smooth(field, rhs, terms, count, fresh):
    for step in range(count):
        if fresh and step == 0:
            field = OMEGA * rhs / terms[7]
        else:
            field = field + OMEGA * (rhs - apply_padded(padded_shard(field), terms)) / terms[7]
    return field


def body(source, coef_x, coef_y, coef_z, absorb):
    side = coef_x.shape[0]
    batch = source.shape[0]
    source = source.reshape(batch, side, side, side)
    coef_x = coef_x.reshape(side, side, side)
    coef_y = coef_y.reshape(side, side, side)
    coef_z = coef_z.reshape(side, side, side)
    absorb = absorb.reshape(side, side, side)
    shapes = []
    kx, ky, kz, sa = (coef_x, coef_y, coef_z, absorb)
    for level in range(LEVELS):
        shapes.append((kx, ky, kz, sa))
        if level + 1 < LEVELS:
            kx, ky, kz, sa = (
                coarsen_coef(kx, 0),
                coarsen_coef(ky, 1),
                coarsen_coef(kz, 2),
                coarsen_cells(sa),
            )
    start = LEVELS - 1
    levels = [shard_terms(*shapes[level]) for level in range(start)]
    rhs = source
    kept = []
    for level in range(start):
        terms = levels[level]
        field = smooth(rhs, rhs, terms, NU, True)
        kept.append((field, rhs))
        rhs = coarsen_cells(rhs - apply_padded(padded_shard(field), terms))
    coarse_terms = shard_terms(*shapes[LEVELS - 1])
    field = smooth(rhs, rhs, coarse_terms, KC, True)
    for level in range(start - 1, -1, -1):
        own, rhs = kept[level]
        field = own + refine_cells(field)
        field = smooth(field, rhs, levels[level], NU, False)
    return field.reshape(batch, side, side * side)


MESH_AXES = ("gx", "gy", "gz")
GATHER_CELLS = 32768
F32 = jnp.float32
BF16 = jnp.bfloat16


def iota2(shape, dim):
    return lax.broadcasted_iota(jnp.int32, shape, dim)


def split_dot(values, selector, transposed=False):
    dims = (((1,), (1,)), ((), ())) if transposed else (((1,), (0,)), ((), ()))
    high = values.astype(BF16)
    rest = values - high.astype(F32)
    low = rest.astype(BF16)

    def one(part):
        return lax.dot_general(part, selector, dims, preferred_element_type=F32)

    return one(high) + one(low)


def selector(lanes, nz, cells, coarse_nz, offset):
    fine = iota2((lanes, 128), 0)
    coarse = iota2((lanes, 128), 1)
    target = (fine // nz // 2) * coarse_nz + (fine % nz) // 2 + offset
    hit = jnp.where((target == coarse) & (fine < cells), 1.0, 0.0)
    return hit.astype(BF16)


def paired_rows(tmp, rows):
    return tmp[pl.ds(0, rows, stride=2), :], tmp[pl.ds(1, rows, stride=2), :]


def doubled_rows(tmp, values):
    rows = values.shape[0]
    tmp[pl.ds(0, rows, stride=2), :] = values
    tmp[pl.ds(1, rows, stride=2), :] = values
    return tmp[0 : 2 * rows, :]


def roll(values, by, axis):
    return pltpu.roll(values, by % values.shape[axis], axis)


def stencil(field, terms, nz):
    lanes = field.shape[1]
    rows = field.shape[0]
    out = terms[0] * pltpu.roll(field, 1, 0) + terms[1] * pltpu.roll(field, rows - 1, 0)
    out = out + (terms[2] * pltpu.roll(field, nz, 1) + terms[3] * pltpu.roll(field, lanes - nz, 1))
    return out + (terms[4] * pltpu.roll(field, 1, 1) + terms[5] * pltpu.roll(field, lanes - 1, 1))


def coarse_coefs(stack, sel, tmp, ny_even, nz_even):
    kx, ky, kz, sa = stack
    rows = kx.shape[0]
    joined = jnp.concatenate([kx, jnp.where(ny_even, ky, 0.0), jnp.where(nz_even, kz, 0.0), sa], axis=0)
    tmp[0 : 4 * rows, :] = split_dot(joined, sel)
    even, odd = paired_rows(tmp, 2 * rows)
    half = rows // 2
    first = even[:half]
    rest = even[half:] + odd[half:]
    return first, rest[:half], rest[half : 2 * half], rest[2 * half :]


def whole_terms(stack, nx, ny, nz):
    kx, ky, kz, sa = stack
    rows, lanes = kx.shape
    x = iota2((rows, lanes), 0)
    lane = iota2((rows, lanes), 1)
    y, z = lane // nz, lane % nz
    real = (x < nx) & (y < ny)
    up_x = jnp.where(x < nx - 1, pltpu.roll(kx, rows - 1, 0), 0.0)
    up_y = jnp.where(y < ny - 1, roll(ky, -nz, 1), 0.0)
    up_z = jnp.where(z < nz - 1, roll(kz, -1, 1), 0.0)
    diag = kx + up_x + ky + up_y + kz + up_z + sa
    weight = jnp.where(real, OMEGA / jnp.where(real, diag, 1.0), 0.0)
    zero = jnp.zeros_like(kx)
    return (
        jnp.where(x > 0, kx * weight, 0.0),
        jnp.where(real, up_x * weight, 0.0),
        jnp.where(y > 0, ky * weight, 0.0),
        jnp.where(real, up_y * weight, 0.0),
        jnp.where(z > 0, kz * weight, 0.0),
        jnp.where(real, up_z * weight, 0.0),
        weight,
        jnp.where(real, diag * (1.0 / OMEGA), zero),
    )


def cycle_kernel(peers, side, batch, src_h, kx_h, ky_h, kz_h, sa_h, out, src, kx_ref, ky_ref, kz_ref, sa_ref, u_s, xs, xr, yr, zs, zr,
                 cxr, cyr, czr, tmp, full, kterms, t1, t2, t3, t4, cfull, back,
                 col, zcol, ccol, czcol, hsend, hrecv, gsend, grecv, lsem):
    gxn, gyn, gzn = peers
    gx, gy, gz = lax.axis_index("gx"), lax.axis_index("gy"), lax.axis_index("gz")
    lanes = side * side
    last = lanes - 128
    MESH = pl.DeviceIdType.MESH

    def at_x(i):
        return (i, gy, gz)

    def at_y(i):
        return (gx, i, gz)

    partner = (gx, gy, 1 - gz)
    others = [at_x(lax.rem(gx + d, gxn)) for d in range(1, gxn)]
    others += [at_y(lax.rem(gy + d, gyn)) for d in range(1, gyn)]
    others += [(lax.rem(gx + d, gxn), gy, 1 - gz) for d in range(gxn)]

    loads = []
    for i, (a, b) in enumerate(((kx_h, kx_ref), (ky_h, ky_ref), (kz_h, kz_ref), (sa_h, sa_ref), (src_h, src))):
        loads.append(pltpu.make_async_copy(a, b, lsem.at[i]))
        loads[i].start()
    xs[...] = jnp.zeros_like(xs)
    xr[...] = jnp.zeros_like(xr)
    yr[...] = jnp.zeros_like(yr)
    cxr[...] = jnp.zeros_like(cxr)
    cyr[...] = jnp.zeros_like(cyr)

    barrier = pltpu.get_barrier_semaphore()
    for peer in others:
        pl.semaphore_signal(barrier, inc=1, device_id=peer, device_id_type=MESH)
    for c in loads:
        c.wait()
    pl.semaphore_wait(barrier, len(others))

    pending = []

    def copy(a, b, s, r, peer):
        return pltpu.make_async_remote_copy(
            src_ref=a, dst_ref=b, send_sem=s, recv_sem=r, device_id=peer, device_id_type=MESH
        )

    def start(c, when=None):
        if when is None:
            c.start()
        else:
            pl.when(when)(c.start)

    def wait(c, kind, when=None):
        run = c.wait_recv if kind == "recv" else c.wait_send
        if when is None:
            run()
        else:
            pl.when(when)(run)

    has_lo_x, has_hi_x = gx > 0, gx < gxn - 1
    has_lo_y, has_hi_y = gy > 0, gy < gyn - 1

    nk = NU * 2 - 1
    c_x = copy(kx_ref.at[0:8], cxr, hsend.at[nk, 0], hrecv.at[nk, 0], at_x(gx - 1))
    c_y = copy(ky_ref.at[:, 0:128], cyr, hsend.at[nk, 1], hrecv.at[nk, 1], at_y(gy - 1))
    c_z = copy(kz_ref, czr, hsend.at[nk, 2], hrecv.at[nk, 2], partner)
    start(c_x, has_lo_x)
    start(c_y, has_lo_y)
    start(c_z)
    pending += [(c_x, has_lo_x), (c_y, has_lo_y), (c_z, None)]

    kx, ky, kz, sa = kx_ref[...], ky_ref[...], kz_ref[...], sa_ref[...]
    x = iota2((side, lanes), 0)
    lane = iota2((side, lanes), 1)
    y, z = lane // side, lane % side
    half = side // 2
    nz1 = half * gzn
    sel0 = selector(lanes, side, lanes, nz1, gz * half)
    fine = iota2((lanes, 128), 0)
    fine_y, fine_z = fine // side, fine % side
    coarse_at = iota2((lanes, 128), 1)

    def picked(hit):
        return jnp.where(hit, 1.0, 0.0).astype(BF16)

    sel_z = picked(
        (fine_z == jnp.where(gz == 0, side - 1, 0))
        & (coarse_at == fine_y // 2 * nz1 + jnp.where(gz == 0, half, half - 1))
    )
    in_row = gz * half + fine_z // 2
    sel_ylo = picked((fine_y == 0) & (coarse_at == (half - 1) * nz1 + in_row))
    sel_yhi = picked((fine_y == side - 1) & (coarse_at == in_row))
    even_y, even_z = (y % 2) == 0, (z % 2) == 0
    coarse = coarse_coefs((kx, ky, kz, sa), sel0, tmp, even_y, even_z)
    mine_x, mine_y = pl.ds(pl.multiple_of(gx * half, half), half), pl.ds(pl.multiple_of(gy * 128, 128), 128)
    for i in range(4):
        ccol[i, mine_x] = coarse[i]

    def gather_xz(mine, other, base):
        cs = []
        for d in range(gxn):
            at = lax.rem(gx + d, gxn)
            ref = mine.at[:, mine_x]
            if d > 0:
                cs.append(copy(ref, ref, gsend.at[base + d], grecv.at[base + d], at_x(at)))
            cs.append(
                copy(ref, other.at[:, mine_x], gsend.at[base + gxn + d], grecv.at[base + gxn + d], (at, gy, 1 - gz))
            )
        for c in cs:
            start(c)
            pending.append((c, None))
        return cs

    def gather_y(whole, base):
        cs = []
        for d in range(1, gyn):
            ref = whole.at[:, :, mine_y]
            cs.append(
                copy(ref, ref, gsend.at[base + 2 * gxn + d], grecv.at[base + 2 * gxn + d], at_y(lax.rem(gy + d, gyn)))
            )
        for c in cs:
            start(c)
            pending.append((c, None))
        return cs

    def landed(cs):
        for c in cs:
            wait(c, "recv")

    cbase = 2 * gxn + gyn
    g = gather_xz(ccol, czcol, cbase)

    wait(c_x, "recv", has_hi_x)
    wait(c_y, "recv", has_hi_y)
    wait(c_z, "recv")

    ylo_mask = (iota2((side, 128), 1) < side)
    yhi_mask = (iota2((side, 128), 1) >= 128 - side)
    first_z, last_z = z == 0, z == side - 1
    up_x = jnp.where(x == side - 1, jnp.broadcast_to(cxr[0:1, :], (side, lanes)), roll(kx, -1, 0))
    from_y = jnp.where(yhi_mask, roll(cyr[...], -side, 1), 0.0)
    up_y = roll(ky, -side, 1)
    up_y = jnp.where(y == side - 1, 0.0, up_y)
    tail = up_y[:, last:] + from_y
    up_y = tail if last == 0 else jnp.concatenate([up_y[:, :last], tail], axis=1)
    low_z = gz == 0
    from_z = jnp.where(low_z, roll(czr[...], side - 1, 1), 0.0)
    up_z = jnp.where(last_z, from_z, roll(kz, -1, 1))
    diag = kx + up_x + ky + up_y + kz + up_z + sa
    weight = OMEGA / diag
    wx, wux, wy, wuy, wz, wuz = [k * weight for k in (kx, up_x, ky, up_y, kz, up_z)]
    inner = (
        jnp.where(x > 0, wx, 0.0),
        jnp.where(x < side - 1, wux, 0.0),
        jnp.where(y > 0, wy, 0.0),
        jnp.where(y < side - 1, wuy, 0.0),
        jnp.where(first_z, 0.0, wz),
        jnp.where(last_z, 0.0, wuz),
    )
    for i in range(6):
        kterms[i] = inner[i]
    kterms[6] = weight
    kterms[7] = diag * (1.0 / OMEGA)
    kterms[8] = jnp.where((x == 0) & has_lo_x, wx, 0.0)
    kterms[9] = jnp.where(x == side - 1, wux, 0.0)
    edge_y = jnp.concatenate(
        [jnp.where(ylo_mask & has_lo_y, wy[:, :128], 0.0), jnp.where(yhi_mask, wuy[:, last:], 0.0)], axis=1
    )
    kterms[10] = edge_y
    kterms[11] = jnp.where(low_z, jnp.where(last_z, wuz, 0.0), jnp.where(first_z, wz, 0.0))

    rhs = [weight * src[r] for r in range(batch)]

    def exchange(k, fields):
        for r in range(batch):
            u_s[k, r] = fields[r]
            xs[k, 0, r : r + 1, :] = fields[r][0:1]
            xs[k, 1, r : r + 1, :] = fields[r][side - 1 : side]
        packed = None
        for r in range(batch):
            moved = pltpu.roll(fields[r], jnp.where(low_z, lanes - (side - 1 - r), side - 1 - r), 1)
            at = jnp.where(low_z, r, side - 1 - r)
            packed = moved if packed is None else jnp.where(z == at, moved, packed)
        zs[k] = packed
        x_lo = copy(xs.at[k, 0], xr.at[k, 1], hsend.at[k, 0], hrecv.at[k, 0], at_x(gx - 1))
        x_hi = copy(xs.at[k, 1], xr.at[k, 0], hsend.at[k, 1], hrecv.at[k, 1], at_x(gx + 1))
        y_lo = copy(u_s.at[k, :, :, 0:128], yr.at[k, 1], hsend.at[k, 2], hrecv.at[k, 2], at_y(gy - 1))
        y_hi = copy(u_s.at[k, :, :, last:lanes], yr.at[k, 0], hsend.at[k, 3], hrecv.at[k, 3], at_y(gy + 1))
        z_to = copy(zs.at[k], zr.at[k], hsend.at[k, 4], hrecv.at[k, 4], partner)
        sent = [(x_lo, has_lo_x), (x_hi, has_hi_x), (y_lo, has_lo_y), (y_hi, has_hi_y), (z_to, None)]
        for c, when in sent:
            start(c, when)
        pending.extend(sent)
        return [(x_lo, has_hi_x), (x_hi, has_lo_x), (y_lo, has_hi_y), (y_hi, has_lo_y), (z_to, None)]

    def moved_by(k, fields, between=None):
        incoming = exchange(k, fields)
        terms = [kterms[i] for i in range(6)]
        acc = [rhs[r] + stencil(fields[r], terms, side) for r in range(batch)]
        if between is not None:
            between()
        for c, when in incoming:
            wait(c, "recv", when)
        state["faces"] = []
        for r in range(batch):
            a = kterms[8] * jnp.broadcast_to(xr[k, 0, r : r + 1, :], (side, lanes))
            a = a + kterms[9] * jnp.broadcast_to(xr[k, 1, r : r + 1, :], (side, lanes))
            ys = jnp.concatenate([roll(yr[k, 0, r], side, 1), roll(yr[k, 1, r], -side, 1)], axis=1)
            a = a + kterms[10] * ys
            zv = pltpu.roll(zr[k], jnp.where(low_z, r, (lanes - r) % lanes), 1) if r else zr[k]
            a = a + kterms[11] * zv
            state["faces"].append(a)
            acc[r] = acc[r] + a
        return acc

    def sweep0(k, fields, between=None):
        acc = moved_by(k, fields, between)
        return [(1.0 - OMEGA) * fields[r] + acc[r] for r in range(batch)]

    state = {}

    def coefs_y():
        landed(g)
        for i in range(4):
            cfull[i, :, mine_y] = ccol[i] + czcol[i]
        state["c"] = gather_y(cfull, cbase)

    nx1, ny1 = gxn * half, gyn * half
    dims = [(nx1 >> i, ny1 >> i, nz1 >> i) for i in range(LEVELS - 1)]
    stores = [t1, t2, t3, t4]
    sels = []

    def coefs_done():
        landed(state["c"])
        stack = tuple(cfull[i] for i in range(4))
        for i, (nx, ny, nz) in enumerate(dims):
            terms = whole_terms(stack, nx, ny, nz)
            for j in range(8):
                stores[i][j] = terms[j]
            if i + 1 < len(dims):
                rows, wide = stack[0].shape
                sel = selector(wide, nz, ny * nz, nz // 2, 0)
                sels.append(sel)
                ln = iota2((rows, wide), 1)
                nxt = coarse_coefs(stack, sel, tmp, (ln // nz) % 2 == 0, (ln % nz) % 2 == 0)
                if nxt[0].shape[0] < 8:
                    pad = jnp.zeros((8 - nxt[0].shape[0], 128), F32)
                    nxt = tuple(jnp.concatenate([a, pad], axis=0) for a in nxt)
                stack = nxt

    u = list(rhs)
    u = sweep0(0, u)
    u = sweep0(1, u, coefs_y)
    acc = moved_by(2, u, coefs_done)
    own0 = u
    faces = state["faces"]
    res = jnp.concatenate([kterms[7] * (acc[r] - OMEGA * u[r]) for r in range(batch)], axis=0)
    tmp[0 : batch * side, :] = split_dot(res, sel0)
    a, b = paired_rows(tmp, batch * half)
    f1 = a + b
    for r in range(batch):
        col[r, mine_x] = f1[r * half : (r + 1) * half]
    landed(gather_xz(col, zcol, 0))
    for r in range(batch):
        full[r, :, mine_y] = col[r] + zcol[r]
    landed(gather_y(full, 0))

    def sweeps(fields, wf, i, count):
        nz = dims[i][2]
        for _ in range(count):
            terms = [stores[i][j] for j in range(6)]
            fields = [
                (1.0 - OMEGA) * fields[r] + (wf[r] + stencil(fields[r], terms, nz)) for r in range(batch)
            ]
        return fields

    f = [full[r] for r in range(batch)]
    kept = []
    for i in range(LEVELS - 2):
        nz = dims[i][2]
        wf = [stores[i][6] * f[r] for r in range(batch)]
        v = sweeps(wf, wf, i, NU - 1)
        kept.append((v, wf))
        terms = [stores[i][j] for j in range(6)]
        res = [
            stores[i][7] * (wf[r] + stencil(v[r], terms, nz) - OMEGA * v[r]) for r in range(batch)
        ]
        rows = res[0].shape[0]
        tmp[0 : batch * rows, :] = split_dot(jnp.concatenate(res, axis=0), sels[i])
        a, b = paired_rows(tmp, batch * rows // 2)
        f1 = a + b
        hr = rows // 2
        f = [f1[r * hr : (r + 1) * hr] for r in range(batch)]
        if hr < 8:
            pad = jnp.zeros((8 - hr, 128), F32)
            f = [jnp.concatenate([p, pad], axis=0) for p in f]
    i = LEVELS - 2
    wf = [stores[i][6] * f[r] for r in range(batch)]
    v = sweeps(wf, wf, i, KC - 1)
    for i in range(LEVELS - 3, -1, -1):
        own, wf = kept[i]
        rows = own[0].shape[0]
        wide = doubled_rows(tmp, jnp.concatenate([v[r][: rows // 2] for r in range(batch)], axis=0))
        up = split_dot(wide, sels[i], transposed=True)
        v = [own[r] + up[r * rows : (r + 1) * rows] for r in range(batch)]
        v = sweeps(v, wf, i, NU)
    for r in range(batch):
        back[r] = v[r]

    def tiles(at_rows, at_lanes):
        return jnp.concatenate([back[r, at_rows, at_lanes] for r in range(batch)], axis=0)

    def rows_at(i):
        return pl.ds(pl.multiple_of(i * half, half), half)

    def lanes_at(i):
        return pl.ds(pl.multiple_of(i * 128, 128), 128)

    below_y, above_y = jnp.maximum(gy - 1, 0), jnp.minimum(gy + 1, gyn - 1)
    part = doubled_rows(tmp, tiles(mine_x, mine_y))
    up = split_dot(part, sel0, transposed=True)
    beside_z = split_dot(part, sel_z, transposed=True)
    edge_lo = doubled_rows(tmp, tiles(mine_x, lanes_at(below_y)))
    edge_hi = doubled_rows(tmp, tiles(mine_x, lanes_at(above_y)))
    beside_y = split_dot(edge_lo, sel_ylo, transposed=True) + split_dot(edge_hi, sel_yhi, transposed=True)
    edge_x = jnp.concatenate(
        [tiles(rows_at(jnp.maximum(gx - 1, 0)), mine_y), tiles(rows_at(jnp.minimum(gx + 1, gxn - 1)), mine_y)], axis=0
    )
    beside_x = split_dot(edge_x, sel0, transposed=True)
    u = []
    terms = [kterms[i] for i in range(6)]
    for r in range(batch):
        v0 = own0[r] + up[r * side : (r + 1) * side]
        lo = beside_x[(r + 1) * half - 1 : (r + 1) * half]
        hi = beside_x[(batch + r) * half : (batch + r) * half + 1]
        a = kterms[8] * jnp.broadcast_to(lo, (side, lanes)) + kterms[9] * jnp.broadcast_to(hi, (side, lanes))
        a = a + kterms[10] * beside_y[r * side : (r + 1) * side]
        a = a + kterms[11] * beside_z[r * side : (r + 1) * side]
        u.append((1.0 - OMEGA) * v0 + (rhs[r] + stencil(v0, terms, side) + faces[r] + a))
    for s in range(1, NU):
        u = sweep0(NU + s - 1, u)
    for r in range(batch):
        out[r] = u[r]
    for c, when in pending:
        wait(c, "send", when)


def kernel_body(peers, source, coef_x, coef_y, coef_z, absorb):
    gxn, gyn, gzn = peers
    batch, side, lanes = source.shape
    half = side // 2
    nx1 = gxn * half
    wide = gyn * half * gzn * half
    ex = 2 * NU - 1
    row_counts = [max(8, nx1 >> i) for i in range(LEVELS - 1)]
    scratch = [
        pltpu.VMEM((batch, side, lanes), F32),
        pltpu.VMEM((side, lanes), F32),
        pltpu.VMEM((side, lanes), F32),
        pltpu.VMEM((side, lanes), F32),
        pltpu.VMEM((side, lanes), F32),
        pltpu.VMEM((ex, batch, side, lanes), F32),
        pltpu.VMEM((ex, 2, 8, lanes), F32),
        pltpu.VMEM((ex, 2, 8, lanes), F32),
        pltpu.VMEM((ex, 2, batch, side, 128), F32),
        pltpu.VMEM((ex, side, lanes), F32),
        pltpu.VMEM((ex, side, lanes), F32),
        pltpu.VMEM((8, lanes), F32),
        pltpu.VMEM((side, 128), F32),
        pltpu.VMEM((side, lanes), F32),
        pltpu.VMEM((4 * nx1 + 64, 128), F32),
        pltpu.VMEM((batch, nx1, wide), F32),
        pltpu.VMEM((12, side, lanes), F32),
        pltpu.VMEM((8, row_counts[0], wide), F32),
        pltpu.VMEM((8, row_counts[1], 128), F32),
        pltpu.VMEM((8, row_counts[2], 128), F32),
        pltpu.VMEM((8, row_counts[3], 128), F32),
        pltpu.VMEM((4, nx1, wide), F32),
        pltpu.VMEM((batch, nx1, wide), F32),
        pltpu.VMEM((batch, nx1, 128), F32),
        pltpu.VMEM((batch, nx1, 128), F32),
        pltpu.VMEM((4, nx1, 128), F32),
        pltpu.VMEM((4, nx1, 128), F32),
        pltpu.SemaphoreType.DMA((ex + 1, 5)),
        pltpu.SemaphoreType.DMA((ex + 1, 5)),
        pltpu.SemaphoreType.DMA((2 * (2 * gxn + gyn),)),
        pltpu.SemaphoreType.DMA((2 * (2 * gxn + gyn),)),
        pltpu.SemaphoreType.DMA((5,)),
    ]
    return pl.pallas_call(
        functools.partial(cycle_kernel, peers, side, batch),
        out_shape=jax.ShapeDtypeStruct(source.shape, F32),
        in_specs=[pl.BlockSpec(memory_space=pl.ANY)] * 5,
        out_specs=pl.BlockSpec(memory_space=pltpu.VMEM),
        scratch_shapes=scratch,
        compiler_params=pltpu.CompilerParams(
            collective_id=0, has_side_effects=True, vmem_limit_bytes=48 * 1024 * 1024
        ),
    )(source, coef_x, coef_y, coef_z, absorb)


def solution(mesh):
    placed = (
        P(None, "gx", ("gy", "gz")),
        P("gx", ("gy", "gz")),
        P("gx", ("gy", "gz")),
        P("gx", ("gy", "gz")),
        P("gx", ("gy", "gz")),
    )
    peers = tuple(mesh.shape[a] for a in MESH_AXES)

    def local(source, coef_x, coef_y, coef_z, absorb):
        side = source.shape[1]
        half = side // 2
        fits = peers[0] * peers[1] * peers[2] * half**3 <= GATHER_CELLS
        fits = fits and peers[2] == 2 and half * half * peers[2] == 128
        if fits:
            return kernel_body(peers, source, coef_x, coef_y, coef_z, absorb)
        return body(source, coef_x, coef_y, coef_z, absorb)

    return jax.shard_map(
        local, mesh=mesh, in_specs=placed, out_specs=P(None, "gx", ("gy", "gz")), check_vma=False
    )
```

```python
import functools

import jax
import jax.numpy as jnp
from jax import lax
from jax.experimental import pallas as pl
from jax.experimental.pallas import tpu as pltpu
from jax.sharding import PartitionSpec as P

LEVELS = 5
NU = 3
KC = 8


OMEGA = 0.8


def passed_along(array, axis, by):
    peers = lax.axis_size(axis)
    pairs = [(i, i + by) for i in range(peers) if 0 <= i + by < peers]
    return lax.ppermute(array, axis, pairs)


def extended(array, sides, width):
    for axis, dim in sides:
        peers, length = (lax.axis_size(axis), array.shape[dim])
        up = [(i, (i + 1) % peers) for i in range(peers - 1)]
        down = [(j, i) for i, j in up]
        last = lax.slice_in_dim(array, length - width, length, axis=dim)
        first = lax.slice_in_dim(array, 0, width, axis=dim)
        before = lax.ppermute(last, axis, up)
        after = lax.ppermute(first, axis, down)
        array = jnp.concatenate([before, array, after], axis=dim)
    return array


def level_terms(coef_x, coef_y, coef_z, absorb, upper_x, upper_y, upper_z):
    diag = coef_x + upper_x + coef_y + upper_y + coef_z + upper_z + absorb
    return (coef_x, upper_x, coef_y, upper_y, coef_z, upper_z, absorb, diag)


def apply_padded(padded, terms):
    coef_x, upper_x, coef_y, upper_y, coef_z, upper_z, absorb, diag = terms
    centre = padded[..., 1:-1, 1:-1, 1:-1]
    out = coef_x * (centre - padded[..., :-2, 1:-1, 1:-1])
    out = out + upper_x * (centre - padded[..., 2:, 1:-1, 1:-1])
    out = out + coef_y * (centre - padded[..., 1:-1, :-2, 1:-1])
    out = out + upper_y * (centre - padded[..., 1:-1, 2:, 1:-1])
    out = out + coef_z * (centre - padded[..., 1:-1, 1:-1, :-2])
    out = out + upper_z * (centre - padded[..., 1:-1, 1:-1, 2:])
    return out + absorb * centre


def coarsen_coef(coef, keep):
    sizes = coef.shape
    blocks = coef.reshape(sizes[0] // 2, 2, sizes[1] // 2, 2, sizes[2] // 2, 2)
    if keep == 0:
        return blocks[:, 0].sum(axis=(2, 4))
    if keep == 1:
        return blocks[:, :, :, 0].sum(axis=(1, 4))
    return blocks[:, :, :, :, :, 0].sum(axis=(1, 3))


def coarsen_cells(field):
    sizes = field.shape
    lead = sizes[:-3]
    blocks = field.reshape(lead + (sizes[-3] // 2, 2, sizes[-2] // 2, 2, sizes[-1] // 2, 2))
    n = len(lead)
    return blocks.sum(axis=(n + 1, n + 3, n + 5))


def refine_cells(field):
    n = field.ndim
    out = jnp.repeat(field, 2, axis=n - 3)
    out = jnp.repeat(out, 2, axis=n - 2)
    return jnp.repeat(out, 2, axis=n - 1)


def shard_terms(kx, ky, kz, absorb):
    plane_x = passed_along(kx[:1], "gx", -1)
    plane_y = passed_along(ky[:, :1], "gy", -1)
    plane_z = passed_along(kz[:, :, :1], "gz", -1)
    upper_x = jnp.concatenate([kx[1:], plane_x], axis=0)
    upper_y = jnp.concatenate([ky[:, 1:], plane_y], axis=1)
    upper_z = jnp.concatenate([kz[:, :, 1:], plane_z], axis=2)
    return level_terms(kx, ky, kz, absorb, upper_x, upper_y, upper_z)


def padded_shard(field):
    return extended(field, (("gx", 1), ("gy", 2), ("gz", 3)), 1)


def smooth(field, rhs, terms, count, fresh):
    for step in range(count):
        if fresh and step == 0:
            field = OMEGA * rhs / terms[7]
        else:
            field = field + OMEGA * (rhs - apply_padded(padded_shard(field), terms)) / terms[7]
    return field


def body(source, coef_x, coef_y, coef_z, absorb):
    side = coef_x.shape[0]
    batch = source.shape[0]
    source = source.reshape(batch, side, side, side)
    coef_x = coef_x.reshape(side, side, side)
    coef_y = coef_y.reshape(side, side, side)
    coef_z = coef_z.reshape(side, side, side)
    absorb = absorb.reshape(side, side, side)
    shapes = []
    kx, ky, kz, sa = (coef_x, coef_y, coef_z, absorb)
    for level in range(LEVELS):
        shapes.append((kx, ky, kz, sa))
        if level + 1 < LEVELS:
            kx, ky, kz, sa = (
                coarsen_coef(kx, 0),
                coarsen_coef(ky, 1),
                coarsen_coef(kz, 2),
                coarsen_cells(sa),
            )
    start = LEVELS - 1
    levels = [shard_terms(*shapes[level]) for level in range(start)]
    rhs = source
    kept = []
    for level in range(start):
        terms = levels[level]
        field = smooth(rhs, rhs, terms, NU, True)
        kept.append((field, rhs))
        rhs = coarsen_cells(rhs - apply_padded(padded_shard(field), terms))
    coarse_terms = shard_terms(*shapes[LEVELS - 1])
    field = smooth(rhs, rhs, coarse_terms, KC, True)
    for level in range(start - 1, -1, -1):
        own, rhs = kept[level]
        field = own + refine_cells(field)
        field = smooth(field, rhs, levels[level], NU, False)
    return field.reshape(batch, side, side * side)


MESH_AXES = ("gx", "gy", "gz")
GATHER_CELLS = 32768
F32 = jnp.float32
BF16 = jnp.bfloat16


def iota2(shape, dim):
    return lax.broadcasted_iota(jnp.int32, shape, dim)


def split_dot(values, selector, transposed=False):
    dims = (((1,), (1,)), ((), ())) if transposed else (((1,), (0,)), ((), ()))
    high = values.astype(BF16)
    rest = values - high.astype(F32)
    low = rest.astype(BF16)

    def one(part):
        return lax.dot_general(part, selector, dims, preferred_element_type=F32)

    return one(high) + one(low)


def selector(lanes, nz, cells, coarse_nz, offset):
    fine = iota2((lanes, 128), 0)
    coarse = iota2((lanes, 128), 1)
    target = (fine // nz // 2) * coarse_nz + (fine % nz) // 2 + offset
    hit = jnp.where((target == coarse) & (fine < cells), 1.0, 0.0)
    return hit.astype(BF16)


def paired_rows(tmp, rows):
    return tmp[pl.ds(0, rows, stride=2), :], tmp[pl.ds(1, rows, stride=2), :]


def doubled_rows(tmp, values):
    rows = values.shape[0]
    tmp[pl.ds(0, rows, stride=2), :] = values
    tmp[pl.ds(1, rows, stride=2), :] = values
    return tmp[0 : 2 * rows, :]


def roll(values, by, axis):
    return pltpu.roll(values, by % values.shape[axis], axis)


def stencil(field, terms, nz):
    lanes = field.shape[1]
    rows = field.shape[0]
    out = terms[0] * pltpu.roll(field, 1, 0) + terms[1] * pltpu.roll(field, rows - 1, 0)
    out = out + (terms[2] * pltpu.roll(field, nz, 1) + terms[3] * pltpu.roll(field, lanes - nz, 1))
    return out + (terms[4] * pltpu.roll(field, 1, 1) + terms[5] * pltpu.roll(field, lanes - 1, 1))


def coarse_coefs(stack, sel, tmp, ny_even, nz_even):
    kx, ky, kz, sa = stack
    rows = kx.shape[0]
    joined = jnp.concatenate([kx, jnp.where(ny_even, ky, 0.0), jnp.where(nz_even, kz, 0.0), sa], axis=0)
    tmp[0 : 4 * rows, :] = split_dot(joined, sel)
    even, odd = paired_rows(tmp, 2 * rows)
    half = rows // 2
    first = even[:half]
    rest = even[half:] + odd[half:]
    return first, rest[:half], rest[half : 2 * half], rest[2 * half :]


def whole_terms(stack, nx, ny, nz):
    kx, ky, kz, sa = stack
    rows, lanes = kx.shape
    x = iota2((rows, lanes), 0)
    lane = iota2((rows, lanes), 1)
    y, z = lane // nz, lane % nz
    real = (x < nx) & (y < ny)
    up_x = jnp.where(x < nx - 1, pltpu.roll(kx, rows - 1, 0), 0.0)
    up_y = jnp.where(y < ny - 1, roll(ky, -nz, 1), 0.0)
    up_z = jnp.where(z < nz - 1, roll(kz, -1, 1), 0.0)
    diag = kx + up_x + ky + up_y + kz + up_z + sa
    weight = jnp.where(real, OMEGA / jnp.where(real, diag, 1.0), 0.0)
    zero = jnp.zeros_like(kx)
    return (
        jnp.where(x > 0, kx * weight, 0.0),
        jnp.where(real, up_x * weight, 0.0),
        jnp.where(y > 0, ky * weight, 0.0),
        jnp.where(real, up_y * weight, 0.0),
        jnp.where(z > 0, kz * weight, 0.0),
        jnp.where(real, up_z * weight, 0.0),
        weight,
        jnp.where(real, diag * (1.0 / OMEGA), zero),
    )


def cycle_kernel(peers, side, batch, src_h, kx_h, ky_h, kz_h, sa_h, out, src, kx_ref, ky_ref, kz_ref, sa_ref, u_s, xs, xr, yr, zs, zr,
                 cxr, cyr, czr, tmp, full, kterms, t1, t2, t3, t4, cfull, back,
                 col, zcol, ccol, czcol, hsend, hrecv, gsend, grecv, lsem):
    gxn, gyn, gzn = peers
    gx, gy, gz = lax.axis_index("gx"), lax.axis_index("gy"), lax.axis_index("gz")
    lanes = side * side
    last = lanes - 128
    MESH = pl.DeviceIdType.MESH

    def at_x(i):
        return (i, gy, gz)

    def at_y(i):
        return (gx, i, gz)

    partner = (gx, gy, 1 - gz)
    others = [at_x(lax.rem(gx + d, gxn)) for d in range(1, gxn)]
    others += [at_y(lax.rem(gy + d, gyn)) for d in range(1, gyn)]
    others += [(lax.rem(gx + d, gxn), gy, 1 - gz) for d in range(gxn)]

    loads = []
    for i, (a, b) in enumerate(((kx_h, kx_ref), (ky_h, ky_ref), (kz_h, kz_ref), (sa_h, sa_ref), (src_h, src))):
        loads.append(pltpu.make_async_copy(a, b, lsem.at[i]))
        loads[i].start()
    xs[...] = jnp.zeros_like(xs)
    xr[...] = jnp.zeros_like(xr)
    yr[...] = jnp.zeros_like(yr)
    cxr[...] = jnp.zeros_like(cxr)
    cyr[...] = jnp.zeros_like(cyr)

    barrier = pltpu.get_barrier_semaphore()
    for peer in others:
        pl.semaphore_signal(barrier, inc=1, device_id=peer, device_id_type=MESH)
    half = side // 2
    nz1 = half * gzn
    sel0 = selector(lanes, side, lanes, nz1, gz * half)
    fine = iota2((lanes, 128), 0)
    fine_y, fine_z = fine // side, fine % side
    coarse_at = iota2((lanes, 128), 1)

    def picked(hit):
        return jnp.where(hit, 1.0, 0.0).astype(BF16)

    sel_z = picked(
        (fine_z == jnp.where(gz == 0, side - 1, 0))
        & (coarse_at == fine_y // 2 * nz1 + jnp.where(gz == 0, half, half - 1))
    )
    in_row = gz * half + fine_z // 2
    sel_ylo = picked((fine_y == 0) & (coarse_at == (half - 1) * nz1 + in_row))
    sel_yhi = picked((fine_y == side - 1) & (coarse_at == in_row))
    nx1, ny1 = gxn * half, gyn * half
    dims = [(nx1 >> i, ny1 >> i, nz1 >> i) for i in range(LEVELS - 1)]
    widths = [ny1 * nz1] + [128] * (LEVELS - 3)
    sels = [
        selector(widths[i], dims[i][2], dims[i][1] * dims[i][2], dims[i][2] // 2, 0) for i in range(LEVELS - 2)
    ]
    for c in loads:
        c.wait()
    pl.semaphore_wait(barrier, len(others))

    pending = []

    def copy(a, b, s, r, peer):
        return pltpu.make_async_remote_copy(
            src_ref=a, dst_ref=b, send_sem=s, recv_sem=r, device_id=peer, device_id_type=MESH
        )

    def start(c, when=None):
        if when is None:
            c.start()
        else:
            pl.when(when)(c.start)

    def wait(c, kind, when=None):
        run = c.wait_recv if kind == "recv" else c.wait_send
        if when is None:
            run()
        else:
            pl.when(when)(run)

    has_lo_x, has_hi_x = gx > 0, gx < gxn - 1
    has_lo_y, has_hi_y = gy > 0, gy < gyn - 1

    nk = NU * 2 - 1
    c_x = copy(kx_ref.at[0:8], cxr, hsend.at[nk, 0], hrecv.at[nk, 0], at_x(gx - 1))
    c_y = copy(ky_ref.at[:, 0:128], cyr, hsend.at[nk, 1], hrecv.at[nk, 1], at_y(gy - 1))
    c_z = copy(kz_ref, czr, hsend.at[nk, 2], hrecv.at[nk, 2], partner)
    start(c_x, has_lo_x)
    start(c_y, has_lo_y)
    start(c_z)
    pending += [(c_x, has_lo_x), (c_y, has_lo_y), (c_z, None)]

    kx, ky, kz, sa = kx_ref[...], ky_ref[...], kz_ref[...], sa_ref[...]
    x = iota2((side, lanes), 0)
    lane = iota2((side, lanes), 1)
    y, z = lane // side, lane % side
    even_y, even_z = (y % 2) == 0, (z % 2) == 0
    coarse = coarse_coefs((kx, ky, kz, sa), sel0, tmp, even_y, even_z)
    mine_x, mine_y = pl.ds(pl.multiple_of(gx * half, half), half), pl.ds(pl.multiple_of(gy * 128, 128), 128)
    for i in range(4):
        ccol[i, mine_x] = coarse[i]

    def gather_xz(mine, other, base):
        cs = []
        for d in range(gxn):
            at = lax.rem(gx + d, gxn)
            ref = mine.at[:, mine_x]
            if d > 0:
                cs.append(copy(ref, ref, gsend.at[base + d], grecv.at[base + d], at_x(at)))
            cs.append(
                copy(ref, other.at[:, mine_x], gsend.at[base + gxn + d], grecv.at[base + gxn + d], (at, gy, 1 - gz))
            )
        for c in cs:
            start(c)
            pending.append((c, None))
        return cs

    def gather_y(whole, base):
        cs = []
        for d in range(1, gyn):
            ref = whole.at[:, :, mine_y]
            cs.append(
                copy(ref, ref, gsend.at[base + 2 * gxn + d], grecv.at[base + 2 * gxn + d], at_y(lax.rem(gy + d, gyn)))
            )
        for c in cs:
            start(c)
            pending.append((c, None))
        return cs

    def landed(cs):
        for c in cs:
            wait(c, "recv")

    cbase = 2 * gxn + gyn
    g = gather_xz(ccol, czcol, cbase)

    wait(c_x, "recv", has_hi_x)
    wait(c_y, "recv", has_hi_y)
    wait(c_z, "recv")

    ylo_mask = (iota2((side, 128), 1) < side)
    yhi_mask = (iota2((side, 128), 1) >= 128 - side)
    first_z, last_z = z == 0, z == side - 1
    up_x = jnp.where(x == side - 1, jnp.broadcast_to(cxr[0:1, :], (side, lanes)), roll(kx, -1, 0))
    from_y = jnp.where(yhi_mask, roll(cyr[...], -side, 1), 0.0)
    up_y = roll(ky, -side, 1)
    up_y = jnp.where(y == side - 1, 0.0, up_y)
    tail = up_y[:, last:] + from_y
    up_y = tail if last == 0 else jnp.concatenate([up_y[:, :last], tail], axis=1)
    low_z = gz == 0
    from_z = jnp.where(low_z, roll(czr[...], side - 1, 1), 0.0)
    up_z = jnp.where(last_z, from_z, roll(kz, -1, 1))
    diag = kx + up_x + ky + up_y + kz + up_z + sa
    weight = OMEGA / diag
    wx, wux, wy, wuy, wz, wuz = [k * weight for k in (kx, up_x, ky, up_y, kz, up_z)]
    inner = (
        jnp.where(x > 0, wx, 0.0),
        jnp.where(x < side - 1, wux, 0.0),
        jnp.where(y > 0, wy, 0.0),
        jnp.where(y < side - 1, wuy, 0.0),
        jnp.where(first_z, 0.0, wz),
        jnp.where(last_z, 0.0, wuz),
    )
    for i in range(6):
        kterms[i] = inner[i]
    kterms[6] = weight
    kterms[7] = diag * (1.0 / OMEGA)
    kterms[8] = jnp.where((x == 0) & has_lo_x, wx, 0.0)
    kterms[9] = jnp.where(x == side - 1, wux, 0.0)
    edge_y = jnp.concatenate(
        [jnp.where(ylo_mask & has_lo_y, wy[:, :128], 0.0), jnp.where(yhi_mask, wuy[:, last:], 0.0)], axis=1
    )
    kterms[10] = edge_y
    kterms[11] = jnp.where(low_z, jnp.where(last_z, wuz, 0.0), jnp.where(first_z, wz, 0.0))

    rhs = [weight * src[r] for r in range(batch)]

    def exchange(k, fields):
        for r in range(batch):
            u_s[k, r] = fields[r]
            xs[k, 0, r : r + 1, :] = fields[r][0:1]
            xs[k, 1, r : r + 1, :] = fields[r][side - 1 : side]
        packed = None
        for r in range(batch):
            moved = pltpu.roll(fields[r], jnp.where(low_z, lanes - (side - 1 - r), side - 1 - r), 1)
            at = jnp.where(low_z, r, side - 1 - r)
            packed = moved if packed is None else jnp.where(z == at, moved, packed)
        zs[k] = packed
        x_lo = copy(xs.at[k, 0], xr.at[k, 1], hsend.at[k, 0], hrecv.at[k, 0], at_x(gx - 1))
        x_hi = copy(xs.at[k, 1], xr.at[k, 0], hsend.at[k, 1], hrecv.at[k, 1], at_x(gx + 1))
        y_lo = copy(u_s.at[k, :, :, 0:128], yr.at[k, 1], hsend.at[k, 2], hrecv.at[k, 2], at_y(gy - 1))
        y_hi = copy(u_s.at[k, :, :, last:lanes], yr.at[k, 0], hsend.at[k, 3], hrecv.at[k, 3], at_y(gy + 1))
        z_to = copy(zs.at[k], zr.at[k], hsend.at[k, 4], hrecv.at[k, 4], partner)
        sent = [(x_lo, has_lo_x), (x_hi, has_hi_x), (y_lo, has_lo_y), (y_hi, has_hi_y), (z_to, None)]
        for c, when in sent:
            start(c, when)
        pending.extend(sent)
        return [(x_lo, has_hi_x), (x_hi, has_lo_x), (y_lo, has_hi_y), (y_hi, has_lo_y), (z_to, None)]

    def moved_by(k, fields, between=None):
        incoming = exchange(k, fields)
        terms = [kterms[i] for i in range(6)]
        acc = [rhs[r] + stencil(fields[r], terms, side) for r in range(batch)]
        if between is not None:
            between()
        for c, when in incoming:
            wait(c, "recv", when)
        state["faces"] = []
        for r in range(batch):
            a = kterms[8] * jnp.broadcast_to(xr[k, 0, r : r + 1, :], (side, lanes))
            a = a + kterms[9] * jnp.broadcast_to(xr[k, 1, r : r + 1, :], (side, lanes))
            ys = jnp.concatenate([roll(yr[k, 0, r], side, 1), roll(yr[k, 1, r], -side, 1)], axis=1)
            a = a + kterms[10] * ys
            zv = pltpu.roll(zr[k], jnp.where(low_z, r, (lanes - r) % lanes), 1) if r else zr[k]
            a = a + kterms[11] * zv
            state["faces"].append(a)
            acc[r] = acc[r] + a
        return acc

    def sweep0(k, fields, between=None):
        acc = moved_by(k, fields, between)
        return [(1.0 - OMEGA) * fields[r] + acc[r] for r in range(batch)]

    state = {}

    def coefs_y():
        landed(g)
        for i in range(4):
            cfull[i, :, mine_y] = ccol[i] + czcol[i]
        state["c"] = gather_y(cfull, cbase)

    stores = [t1, t2, t3, t4]

    def coefs_done():
        landed(state["c"])
        stack = tuple(cfull[i] for i in range(4))
        for i, (nx, ny, nz) in enumerate(dims):
            terms = whole_terms(stack, nx, ny, nz)
            for j in range(8):
                stores[i][j] = terms[j]
            if i + 1 < len(dims):
                rows, wide = stack[0].shape
                sel = sels[i]
                ln = iota2((rows, wide), 1)
                nxt = coarse_coefs(stack, sel, tmp, (ln // nz) % 2 == 0, (ln % nz) % 2 == 0)
                if nxt[0].shape[0] < 8:
                    pad = jnp.zeros((8 - nxt[0].shape[0], 128), F32)
                    nxt = tuple(jnp.concatenate([a, pad], axis=0) for a in nxt)
                stack = nxt

    u = list(rhs)
    u = sweep0(0, u)
    u = sweep0(1, u, coefs_y)
    acc = moved_by(2, u, coefs_done)
    own0 = u
    faces = state["faces"]
    res = jnp.concatenate([kterms[7] * (acc[r] - OMEGA * u[r]) for r in range(batch)], axis=0)
    tmp[0 : batch * side, :] = split_dot(res, sel0)
    a, b = paired_rows(tmp, batch * half)
    f1 = a + b
    for r in range(batch):
        col[r, mine_x] = f1[r * half : (r + 1) * half]
    landed(gather_xz(col, zcol, 0))
    for r in range(batch):
        full[r, :, mine_y] = col[r] + zcol[r]
    landed(gather_y(full, 0))

    def sweeps(fields, wf, i, count):
        nz = dims[i][2]
        for _ in range(count):
            terms = [stores[i][j] for j in range(6)]
            fields = [
                (1.0 - OMEGA) * fields[r] + (wf[r] + stencil(fields[r], terms, nz)) for r in range(batch)
            ]
        return fields

    f = [full[r] for r in range(batch)]
    kept = []
    for i in range(LEVELS - 2):
        nz = dims[i][2]
        wf = [stores[i][6] * f[r] for r in range(batch)]
        v = sweeps(wf, wf, i, NU - 1)
        kept.append((v, wf))
        terms = [stores[i][j] for j in range(6)]
        res = [
            stores[i][7] * (wf[r] + stencil(v[r], terms, nz) - OMEGA * v[r]) for r in range(batch)
        ]
        rows = res[0].shape[0]
        tmp[0 : batch * rows, :] = split_dot(jnp.concatenate(res, axis=0), sels[i])
        a, b = paired_rows(tmp, batch * rows // 2)
        f1 = a + b
        hr = rows // 2
        f = [f1[r * hr : (r + 1) * hr] for r in range(batch)]
        if hr < 8:
            pad = jnp.zeros((8 - hr, 128), F32)
            f = [jnp.concatenate([p, pad], axis=0) for p in f]
    i = LEVELS - 2
    wf = [stores[i][6] * f[r] for r in range(batch)]
    v = sweeps(wf, wf, i, KC - 1)
    for i in range(LEVELS - 3, -1, -1):
        own, wf = kept[i]
        rows = own[0].shape[0]
        wide = doubled_rows(tmp, jnp.concatenate([v[r][: rows // 2] for r in range(batch)], axis=0))
        up = split_dot(wide, sels[i], transposed=True)
        v = [own[r] + up[r * rows : (r + 1) * rows] for r in range(batch)]
        v = sweeps(v, wf, i, NU)
    for r in range(batch):
        back[r] = v[r]

    def tiles(at_rows, at_lanes):
        return jnp.concatenate([back[r, at_rows, at_lanes] for r in range(batch)], axis=0)

    def rows_at(i):
        return pl.ds(pl.multiple_of(i * half, half), half)

    def lanes_at(i):
        return pl.ds(pl.multiple_of(i * 128, 128), 128)

    below_y, above_y = jnp.maximum(gy - 1, 0), jnp.minimum(gy + 1, gyn - 1)
    part = doubled_rows(tmp, tiles(mine_x, mine_y))
    up = split_dot(part, sel0, transposed=True)
    beside_z = split_dot(part, sel_z, transposed=True)
    edge_lo = doubled_rows(tmp, tiles(mine_x, lanes_at(below_y)))
    edge_hi = doubled_rows(tmp, tiles(mine_x, lanes_at(above_y)))
    beside_y = split_dot(edge_lo, sel_ylo, transposed=True) + split_dot(edge_hi, sel_yhi, transposed=True)
    edge_x = jnp.concatenate(
        [tiles(rows_at(jnp.maximum(gx - 1, 0)), mine_y), tiles(rows_at(jnp.minimum(gx + 1, gxn - 1)), mine_y)], axis=0
    )
    beside_x = split_dot(edge_x, sel0, transposed=True)
    u = []
    terms = [kterms[i] for i in range(6)]
    for r in range(batch):
        v0 = own0[r] + up[r * side : (r + 1) * side]
        lo = beside_x[(r + 1) * half - 1 : (r + 1) * half]
        hi = beside_x[(batch + r) * half : (batch + r) * half + 1]
        a = kterms[8] * jnp.broadcast_to(lo, (side, lanes)) + kterms[9] * jnp.broadcast_to(hi, (side, lanes))
        a = a + kterms[10] * beside_y[r * side : (r + 1) * side]
        a = a + kterms[11] * beside_z[r * side : (r + 1) * side]
        u.append((1.0 - OMEGA) * v0 + (rhs[r] + stencil(v0, terms, side) + faces[r] + a))
    for s in range(1, NU):
        u = sweep0(NU + s - 1, u)
    for r in range(batch):
        out[r] = u[r]
    for c, when in pending:
        wait(c, "send", when)


def kernel_body(peers, source, coef_x, coef_y, coef_z, absorb):
    gxn, gyn, gzn = peers
    batch, side, lanes = source.shape
    half = side // 2
    nx1 = gxn * half
    wide = gyn * half * gzn * half
    ex = 2 * NU - 1
    row_counts = [max(8, nx1 >> i) for i in range(LEVELS - 1)]
    scratch = [
        pltpu.VMEM((batch, side, lanes), F32),
        pltpu.VMEM((side, lanes), F32),
        pltpu.VMEM((side, lanes), F32),
        pltpu.VMEM((side, lanes), F32),
        pltpu.VMEM((side, lanes), F32),
        pltpu.VMEM((ex, batch, side, lanes), F32),
        pltpu.VMEM((ex, 2, 8, lanes), F32),
        pltpu.VMEM((ex, 2, 8, lanes), F32),
        pltpu.VMEM((ex, 2, batch, side, 128), F32),
        pltpu.VMEM((ex, side, lanes), F32),
        pltpu.VMEM((ex, side, lanes), F32),
        pltpu.VMEM((8, lanes), F32),
        pltpu.VMEM((side, 128), F32),
        pltpu.VMEM((side, lanes), F32),
        pltpu.VMEM((4 * nx1 + 64, 128), F32),
        pltpu.VMEM((batch, nx1, wide), F32),
        pltpu.VMEM((12, side, lanes), F32),
        pltpu.VMEM((8, row_counts[0], wide), F32),
        pltpu.VMEM((8, row_counts[1], 128), F32),
        pltpu.VMEM((8, row_counts[2], 128), F32),
        pltpu.VMEM((8, row_counts[3], 128), F32),
        pltpu.VMEM((4, nx1, wide), F32),
        pltpu.VMEM((batch, nx1, wide), F32),
        pltpu.VMEM((batch, nx1, 128), F32),
        pltpu.VMEM((batch, nx1, 128), F32),
        pltpu.VMEM((4, nx1, 128), F32),
        pltpu.VMEM((4, nx1, 128), F32),
        pltpu.SemaphoreType.DMA((ex + 1, 5)),
        pltpu.SemaphoreType.DMA((ex + 1, 5)),
        pltpu.SemaphoreType.DMA((2 * (2 * gxn + gyn),)),
        pltpu.SemaphoreType.DMA((2 * (2 * gxn + gyn),)),
        pltpu.SemaphoreType.DMA((5,)),
    ]
    return pl.pallas_call(
        functools.partial(cycle_kernel, peers, side, batch),
        out_shape=jax.ShapeDtypeStruct(source.shape, F32),
        in_specs=[pl.BlockSpec(memory_space=pltpu.HBM)] * 5,
        out_specs=pl.BlockSpec(memory_space=pltpu.VMEM),
        scratch_shapes=scratch,
        compiler_params=pltpu.CompilerParams(
            collective_id=0, has_side_effects=True, vmem_limit_bytes=48 * 1024 * 1024
        ),
    )(source, coef_x, coef_y, coef_z, absorb)


def solution(mesh):
    placed = (
        P(None, "gx", ("gy", "gz")),
        P("gx", ("gy", "gz")),
        P("gx", ("gy", "gz")),
        P("gx", ("gy", "gz")),
        P("gx", ("gy", "gz")),
    )
    peers = tuple(mesh.shape[a] for a in MESH_AXES)

    def local(source, coef_x, coef_y, coef_z, absorb):
        side = source.shape[1]
        half = side // 2
        fits = peers[0] * peers[1] * peers[2] * half**3 <= GATHER_CELLS
        fits = fits and peers[2] == 2 and half * half * peers[2] == 128
        if fits:
            return kernel_body(peers, source, coef_x, coef_y, coef_z, absorb)
        return body(source, coef_x, coef_y, coef_z, absorb)

    return jax.shard_map(
        local, mesh=mesh, in_specs=placed, out_specs=P(None, "gx", ("gy", "gz")), check_vma=False
    )
```
